32 devices in a mesh: own: 4 (over y, x), br: 8 (over z, core).
Axes of the slice: x: 2, y: 2, z: 4, core: 2. Of those that a mesh axis runs over, the one named last changes fastest.
Arguments:
- queries: bfloat16 [32, 256, 5120], P('br', None, 'own'), may hold values from -6 to 6
- branch_keys: bfloat16 [32, 256, 1024], P('br', None, 'own'), may hold values from -6 to 6
- branch_values: bfloat16 [32, 256, 1024], P('br', None, 'own'), may hold values from -6 to 6
- attn_out: bfloat16 [32, 256, 5120], P('br', None, 'own'), may hold values from -6 to 6
- out_grad: bfloat16 [32, 256, 5120], P('br', None, 'own'), may hold values from -6 to 6
- logsumexp: float32 [32, 40, 256], P('br', 'own'), may hold values from 7 to 8.5
- prefix_keys: bfloat16 [512, 4, 1024], P('br', 'own'), may hold values from -6 to 6
- prefix_values: bfloat16 [512, 4, 1024], P('br', 'own'), may hold values from -6 to 6
- prefix_of: int32 [32], P('br'), may hold values from 0 to 3
- counts: int32 [8], P('br'), may hold values from 1 to 4, as said below
Outputs:
- query_grad: bfloat16 [32, 256, 5120], P('br', None, 'own')
- key_grad: bfloat16 [32, 256, 1024], P('br', None, 'own')
- value_grad: bfloat16 [32, 256, 1024], P('br', None, 'own')
- prefix_key_grad: bfloat16 [512, 4, 1024], P('br', 'own')
- prefix_value_grad: bfloat16 [512, 4, 1024], P('br', 'own')
The draws below stay inside these ranges and needn't reach their ends.
Inputs may be any that keep to these rules, and one draw needn't show every extreme that they name: The first counts[b] of the 4 slots of br index b hold branches, the other slots are empty; some br index is full in every draw.
All inputs are finite; a program needn't handle non-finite values.
Results may differ from the reference program's by a relative error of at most 0.0049.
Values may be sent and summed in bfloat16 or wider, within the bound.
A program may use at most 64 MiB of HBM per device.

```python
import jax
import jax.numpy as jnp
from jax import lax

QH = 40
KVH = 8
HD = 128
CAP = 4
L = 256
P_SIZE = 512
NPRE = 4
SLOTS = 32
N_BR = 8


def draw_counts(key, part):
    key = jax.random.fold_in(key, 7)
    first, second = jax.random.split(key)
    picks = jax.random.randint(first, (N_BR,), 0, 4)
    values = jnp.where(picks == 0, CAP, 1).astype(jnp.int32)
    full_at = jax.random.randint(second, (), 0, N_BR)
    return values.at[full_at].set(CAP)


def with_ends(drawn, rng, least, high):
    longest = drawn.shape.index(max(drawn.shape))
    spots = []
    for shift in (0, 1):
        where = [jax.random.randint(jax.random.fold_in(rng, axis), (), 0, length) for axis, length in enumerate(drawn.shape)]
        where[longest] = (where[longest] + shift) % drawn.shape[longest]
        spots.append(tuple(where))
    return drawn.at[spots[0]].set(least).at[spots[1]].set(high)


def shard_levels(own_key, dims, cuts, low, largest):
    loudness, own = 1.0, jax.random.fold_in(own_key, 6)
    for dim, parts in cuts:
        heights = jnp.exp(jax.random.uniform(jax.random.fold_in(own, dim), (parts,), jnp.float32, low / len(cuts), largest / len(cuts)))
        loudness = loudness * jnp.repeat(heights, dims[dim] // parts).reshape([-1 if axis == dim else 1 for axis in range(len(dims))])
    return loudness


def normal_values(own_key, extent, width, bound, cuts=(), kind=jnp.bfloat16):
    array = width * jax.random.normal(own_key, extent, jnp.float32)
    if cuts:
        array = array * shard_levels(own_key, extent, cuts, -0.22, 0.18)
    return jnp.clip(array, -bound, bound).astype(kind)


def setup_inputs(seed: int = 0) -> dict:
    key_of = jax.random.split(jax.random.key(seed), 11)
    queries = normal_values(key_of[0], (SLOTS, L, QH * HD), 1.2, 6.0, ((0, 8), (2, 4)))
    branch_keys = normal_values(key_of[1], (SLOTS, L, KVH * HD), 1.2, 6.0, ((0, 8), (2, 4)))
    branch_values = normal_values(key_of[2], (SLOTS, L, KVH * HD), 1.0, 6.0, ((0, 8), (2, 4)))
    attn_out = normal_values(key_of[3], (SLOTS, L, QH * HD), 1.0, 6.0, ((0, 8), (2, 4)))
    out_grad = normal_values(key_of[4], (SLOTS, L, QH * HD), 2.0, 6.0, ((0, 8), (2, 4)))
    logsumexp = jnp.clip(7.0 + 1.5 * jax.random.uniform(key_of[5], (SLOTS, QH, L), jnp.float32) ** shard_levels(key_of[5], (SLOTS, QH, L), ((0, 8), (1, 4)), -0.2, 0.2), 7.0, 8.5)
    prefix_keys = normal_values(key_of[6], (P_SIZE, NPRE, KVH * HD), 1.2, 6.0, ((0, 8), (1, 4)))
    prefix_values = normal_values(key_of[7], (P_SIZE, NPRE, KVH * HD), 1.0, 6.0, ((0, 8), (1, 4)))
    prefix_of = with_ends(jax.random.randint(key_of[8], (SLOTS,), 0, NPRE), jax.random.fold_in(key_of[8], 1), 0, NPRE - 1).astype(jnp.int32)
    counts = draw_counts(jax.random.fold_in(key_of[10], 71), 0)
    return dict(queries=queries, branch_keys=branch_keys, branch_values=branch_values, attn_out=attn_out, out_grad=out_grad, logsumexp=logsumexp, prefix_keys=prefix_keys, prefix_values=prefix_values, prefix_of=prefix_of, counts=counts)


def reference(queries, branch_keys, branch_values, attn_out, out_grad, logsumexp, prefix_keys, prefix_values, prefix_of, counts):
    groups = QH // KVH
    scale = HD ** -0.5
    slot_ids = jnp.arange(SLOTS, dtype=jnp.int32)
    alive = ((slot_ids % CAP) < counts[slot_ids // CAP]).astype(jnp.float32)
    rows = jnp.arange(P_SIZE + L, dtype=jnp.int32)[None, :]
    tokens = jnp.arange(L, dtype=jnp.int32)[:, None]
    visible = (rows < P_SIZE) | (rows - P_SIZE <= tokens)

    def step(carry, item):
        pk_acc, pv_acc = carry
        query, bkey, bval, out, dout, lse, pidx, live = item
        pkey = lax.dynamic_index_in_dim(prefix_keys, pidx, 1, keepdims=False)
        pval = lax.dynamic_index_in_dim(prefix_values, pidx, 1, keepdims=False)
        all_keys = jnp.concatenate([pkey, bkey], 0).astype(jnp.float32).reshape(P_SIZE + L, KVH, HD)
        all_vals = jnp.concatenate([pval, bval], 0).astype(jnp.float32).reshape(P_SIZE + L, KVH, HD)
        q4 = query.astype(jnp.float32).reshape(L, KVH, groups, HD)
        d4 = dout.astype(jnp.float32).reshape(L, KVH, groups, HD)
        o4 = out.astype(jnp.float32).reshape(L, KVH, groups, HD)
        delta = jnp.einsum('lkgd,lkgd->kgl', d4, o4)
        score = jnp.einsum('lkgd,rkd->kglr', q4, all_keys) * scale
        lse4 = lse.reshape(KVH, groups, L)
        prob = jnp.where(visible, jnp.exp(score - lse4[..., None]), 0.0) * live
        prob_b = prob.astype(jnp.bfloat16).astype(jnp.float32)
        dprob = jnp.einsum('lkgd,rkd->kglr', d4, all_vals)
        dscore = (prob * (dprob - delta[..., None])).astype(jnp.bfloat16).astype(jnp.float32)
        dq = scale * jnp.einsum('kglr,rkd->lkgd', dscore, all_keys)
        dk = scale * jnp.einsum('kglr,lkgd->rkd', dscore, q4).reshape(P_SIZE + L, KVH * HD)
        dv = jnp.einsum('kglr,lkgd->rkd', prob_b, d4).reshape(P_SIZE + L, KVH * HD)
        old_k = lax.dynamic_index_in_dim(pk_acc, pidx, 1, keepdims=False)
        old_v = lax.dynamic_index_in_dim(pv_acc, pidx, 1, keepdims=False)
        pk_acc = lax.dynamic_update_index_in_dim(pk_acc, old_k + dk[:P_SIZE], pidx, 1)
        pv_acc = lax.dynamic_update_index_in_dim(pv_acc, old_v + dv[:P_SIZE], pidx, 1)
        outs = (dq.reshape(L, QH * HD).astype(jnp.bfloat16), dk[P_SIZE:].astype(jnp.bfloat16), dv[P_SIZE:].astype(jnp.bfloat16))
        return (pk_acc, pv_acc), outs

    zeros = jnp.zeros((P_SIZE, NPRE, KVH * HD), jnp.float32)
    items = (queries, branch_keys, branch_values, attn_out, out_grad, logsumexp, prefix_of, alive)
    (pk_acc, pv_acc), (dq_all, dk_all, dv_all) = lax.scan(step, (zeros, zeros), items)
    return dq_all, dk_all, dv_all, pk_acc.astype(jnp.bfloat16), pv_acc.astype(jnp.bfloat16)
```

```python
import functools

import jax
import jax.numpy as jnp
from jax import lax
from jax.experimental import pallas as pl
from jax.experimental.pallas import tpu as pltpu
from jax.sharding import PartitionSpec as P

QH = 40
KVH = 8
HD = 128
GROUPS = QH // KVH
LOG2E = 1.4426950408889634
SCALE = HD ** (-0.5)
DEAD = 1e30

MESH = pl.DeviceIdType.MESH


def flip(index, bits):
    out, bit = index, 1
    while bit <= bits:
        if bits & bit:
            out = out + bit * (1 - 2 * ((index // bit) % 2))
        bit *= 2
    return out


def dot_nt(a, b):
    return lax.dot_general(a, b, (((1,), (1,)), ((), ())), preferred_element_type=jnp.float32)


def dot(a, b):
    return jnp.dot(a, b, preferred_element_type=jnp.float32)


def kernel(
    n_own,
    planes,
    pref_ref,
    w_ref,
    src,
    q_ref,
    bk_ref,
    bv_ref,
    ao_ref,
    og_ref,
    lse_ref,
    qg_ref,
    kg_ref,
    vg_ref,
    pk_ref,
    pv_ref,
    g0,
    g1,
    dqt,
    delta,
    acc,
    mine0,
    mine1,
    out0,
    out1,
    in0,
    in1,
    pre0,
    pre1,
    land,
    g_send,
    g_recv,
    f_send,
    f_recv,
    local_sem,
    s_send,
    s_recv,
    r_send,
    r_recv,
):
    slots, length, _ = q_ref.shape
    kv_heads = bk_ref.shape[2] // HD
    cw = kv_heads * HD
    ppo, rows = src.shape[1], src.shape[2]
    num_pre = n_own * ppo
    half = planes // 2
    chunk_rows = half * 2 * rows
    own = lax.axis_index("own")
    br = lax.axis_index("br")
    plane, core = br // 2, br % 2
    gathered, mine, outgoing, incoming, presum = (
        (g0, g1),
        (mine0, mine1),
        (out0, out1),
        (in0, in1),
        (pre0, pre1),
    )

    def device(d, j):
        return {"own": flip(own, j), "br": flip(plane, d) * 2 + core}

    sibling = {"own": own, "br": plane * 2 + 1 - core}
    peers = [(d, j) for d in range(planes) for j in range(n_own) if (d, j) != (0, 0)]

    barrier = pltpu.get_barrier_semaphore()
    for d, j in peers:
        pl.semaphore_signal(barrier, inc=1, device_id=device(d, j), device_id_type=MESH)
    pl.semaphore_signal(barrier, inc=1, device_id=sibling, device_id_type=MESH)
    pl.semaphore_wait(barrier, len(peers) + 1)

    def place(d, o, side):
        return gathered[d // half].at[pl.ds(o * ppo, ppo), 2 * (d % half) + side]

    def gather_copy(d, j):
        return pltpu.make_async_remote_copy(
            src_ref=src.at[flip(own, j)],
            dst_ref=place(d, own, 0),
            send_sem=g_send.at[d, j],
            recv_sem=g_recv.at[d, j],
            device_id=device(d, j),
            device_id_type=MESH,
        )

    def forward_copy(d, j):
        o = flip(own, j)
        return pltpu.make_async_remote_copy(
            src_ref=src.at[own] if (d, j) == (0, 0) else place(d, o, 0),
            dst_ref=place(d, o, 1),
            send_sem=f_send.at[d, j],
            recv_sem=f_recv.at[d, j],
            device_id=sibling,
            device_id_type=MESH,
        )

    local = pltpu.make_async_copy(src.at[own], place(0, own, 0), local_sem)
    local.start()
    for d, j in reversed(peers):
        gather_copy(d, j).start()
    forward_copy(0, 0).start()

    def head_cols(k, h):
        return pl.ds(pl.multiple_of(k * (GROUPS * HD) + h * HD, HD), HD)

    def kv_cols(k, base):
        return pl.ds(pl.multiple_of(base + k * HD, HD), HD)

    def grads(c, k, key, val, causal, use_dq):
        key_t = key.T
        dk = dv = None
        for h in range(GROUPS):
            query = q_ref[c, :, head_cols(k, h)]
            grad = og_ref[c, :, head_cols(k, h)]
            lse = lse_ref[c, k, pl.ds(h, 1), :]
            if causal is not None:
                product = grad.astype(jnp.float32) * ao_ref[c, :, head_cols(k, h)].astype(
                    jnp.float32
                )
                dlt = jnp.sum(product.T, axis=0, keepdims=True)
                delta[c, k, pl.ds(h, 1), :] = dlt
            else:
                dlt = delta[c, k, pl.ds(h, 1), :]
            prob = jnp.exp2(dot_nt(key, query) * (SCALE * LOG2E) - lse)
            if causal is not None:
                prob = jnp.where(causal, prob, 0.0)
            dscore = (prob * (dot_nt(val, grad) - dlt)).astype(jnp.bfloat16)
            dk_h = dot(dscore, query)
            dv_h = dot(prob.astype(jnp.bfloat16), grad)
            dk = dk_h if dk is None else dk + dk_h
            dv = dv_h if dv is None else dv + dv_h
            use_dq(h, dot(key_t, dscore))
        return dk * SCALE, dv

    causal = lax.broadcasted_iota(jnp.int32, (length, length), 0) <= lax.broadcasted_iota(
        jnp.int32, (length, length), 1
    )

    def branch_step(step, carry):
        c, k = step // kv_heads, step % kv_heads

        def use_dq(h, term):
            dqt[c, k, h] = term

        dk, dv = grads(
            c, k, bk_ref[c, :, kv_cols(k, 0)], bv_ref[c, :, kv_cols(k, 0)], causal, use_dq
        )
        kg_ref[c, :, kv_cols(k, 0)] = dk.astype(jnp.bfloat16)
        vg_ref[c, :, kv_cols(k, 0)] = dv.astype(jnp.bfloat16)
        return carry

    lax.fori_loop(0, slots * kv_heads, branch_step, 0)

    def arrive(chunk):
        here = [(d, j) for d, j in peers if d // half == chunk]
        for d, j in here:
            gather_copy(d, j).wait_recv()
            forward_copy(d, j).start()
        if chunk == 0:
            local.wait()
            here = here + [(0, 0)]
        for d, j in here:
            forward_copy(d, j).wait_recv()

    def prefix_chunk(chunk):
        buf = gathered[chunk]

        def prefix_step(step, carry):
            c, k = step // kv_heads, step % kv_heads
            p = pref_ref[c]
            key = buf[p, :, :, kv_cols(k, 0)].reshape(chunk_rows, HD)
            val = buf[p, :, :, kv_cols(k, cw)].reshape(chunk_rows, HD)

            def use_dq(h, term):
                total = dqt[c, k, h] + term
                if chunk == 0:
                    dqt[c, k, h] = total
                else:
                    qg_ref[c, :, head_cols(k, h)] = (total * SCALE).T.astype(jnp.bfloat16)

            dk, dv = grads(c, k, key, val, None, use_dq)
            acc[c, :, kv_cols(k, 0)] = dk
            acc[c, :, kv_cols(k, cw)] = dv
            return carry

        lax.fori_loop(0, slots * kv_heads, prefix_step, 0)

        def combine(dd, carry):
            for side, target in ((0, mine[chunk]), (1, outgoing[chunk])):
                start = pl.multiple_of((dd * 2 + side) * rows, rows)
                parts = [acc[c, pl.ds(start, rows), :] for c in range(slots)]
                for p in range(num_pre):
                    total = parts[0] * w_ref[0, p]
                    for c in range(1, slots):
                        total = total + parts[c] * w_ref[c, p]
                    target[dd, p] = total.astype(target.dtype)
            return carry

        lax.fori_loop(0, half, combine, 0)

    def sibling_copy(chunk):
        return pltpu.make_async_remote_copy(
            src_ref=outgoing[chunk],
            dst_ref=incoming[chunk],
            send_sem=s_send.at[chunk],
            recv_sem=s_recv.at[chunk],
            device_id=sibling,
            device_id_type=MESH,
        )

    def reduce_copy(d, j):
        return pltpu.make_async_remote_copy(
            src_ref=presum[d // half].at[d % half, pl.ds(flip(own, j) * ppo, ppo)],
            dst_ref=land.at[d, own],
            send_sem=r_send.at[d, j],
            recv_sem=r_recv.at[d, j],
            device_id=device(d, j),
            device_id_type=MESH,
        )

    def send_sums(chunk):
        sibling_copy(chunk).wait_recv()

        def add(dd, carry):
            for p in range(num_pre):
                presum[chunk][dd, p] = (
                    mine[chunk][dd, p] + incoming[chunk][dd, p].astype(jnp.float32)
                ).astype(jnp.bfloat16)
            return carry

        lax.fori_loop(0, half, add, 0)
        for d, j in reversed(peers):
            if d // half == chunk:
                reduce_copy(d, j).start()
        if chunk == 0:
            land[0, own] = presum[0][0, pl.ds(own * ppo, ppo)]

    arrive(0)
    prefix_chunk(0)
    sibling_copy(0).start()
    arrive(1)
    send_sums(0)
    prefix_chunk(1)
    sibling_copy(1).start()
    send_sums(1)

    for d, j in peers:
        reduce_copy(d, j).wait_recv()

    for o in range(n_own):
        for i in range(ppo):
            total = land[0, o, i].astype(jnp.float32)
            for d in range(1, planes):
                total = total + land[d, o, i].astype(jnp.float32)
            pk_ref[i, :, o * cw : (o + 1) * cw] = total[:, :cw].astype(jnp.bfloat16)
            pv_ref[i, :, o * cw : (o + 1) * cw] = total[:, cw:].astype(jnp.bfloat16)

    forward_copy(0, 0).wait_send()
    for d, j in peers:
        gather_copy(d, j).wait_send()
        forward_copy(d, j).wait_send()
        reduce_copy(d, j).wait_send()
    for chunk in (0, 1):
        sibling_copy(chunk).wait_send()


def per_device(
    queries,
    branch_keys,
    branch_values,
    attn_out,
    out_grad,
    logsumexp,
    prefix_keys,
    prefix_values,
    prefix_of,
    counts,
    *,
    n_own,
    n_br,
):
    slots, length, width = queries.shape
    cw = branch_keys.shape[2]
    kv_heads = cw // HD
    rows, ppo, _ = prefix_keys.shape
    num_pre = n_own * ppo
    planes = n_br // 2
    half = planes // 2
    alive = jnp.arange(slots) < counts[0]
    lse = jnp.where(alive[:, None, None], logsumexp * LOG2E, DEAD).reshape(
        slots, kv_heads, GROUPS, length
    )
    weights = (prefix_of[:, None] == jnp.arange(num_pre)[None, :]).astype(jnp.float32)
    kv = jnp.concatenate(
        [
            prefix_keys.reshape(rows, ppo, n_own, cw),
            prefix_values.reshape(rows, ppo, n_own, cw),
        ],
        axis=3,
    ).transpose(2, 1, 0, 3)

    bf16, f32 = jnp.bfloat16, jnp.float32
    vmem = pl.BlockSpec(memory_space=pltpu.VMEM)
    smem = pl.BlockSpec(memory_space=pltpu.SMEM)
    dma = pltpu.SemaphoreType.DMA
    part = (half, num_pre, rows, 2 * cw)
    query_grad, key_grad, value_grad, pk, pv = pl.pallas_call(
        functools.partial(kernel, n_own, planes),
        out_shape=(
            jax.ShapeDtypeStruct(queries.shape, bf16),
            jax.ShapeDtypeStruct(branch_keys.shape, bf16),
            jax.ShapeDtypeStruct(branch_keys.shape, bf16),
            jax.ShapeDtypeStruct((ppo, rows, n_own * cw), bf16),
            jax.ShapeDtypeStruct((ppo, rows, n_own * cw), bf16),
        ),
        in_specs=[smem, smem] + [vmem] * 7,
        out_specs=(vmem,) * 5,
        scratch_shapes=[
            pltpu.VMEM((num_pre, planes, rows, 2 * cw), bf16),
            pltpu.VMEM((num_pre, planes, rows, 2 * cw), bf16),
            pltpu.VMEM((slots, kv_heads, GROUPS, HD, length), f32),
            pltpu.VMEM((slots, kv_heads, GROUPS, length), f32),
            pltpu.VMEM((slots, planes * rows, 2 * cw), f32),
            pltpu.VMEM(part, f32),
            pltpu.VMEM(part, f32),
            pltpu.VMEM(part, bf16),
            pltpu.VMEM(part, bf16),
            pltpu.VMEM(part, bf16),
            pltpu.VMEM(part, bf16),
            pltpu.VMEM(part, bf16),
            pltpu.VMEM(part, bf16),
            pltpu.VMEM((planes, n_own, ppo, rows, 2 * cw), bf16),
            dma((planes, n_own)),
            dma((planes, n_own)),
            dma((planes, n_own)),
            dma((planes, n_own)),
            dma(()),
            dma((2,)),
            dma((2,)),
            dma((planes, n_own)),
            dma((planes, n_own)),
        ],
        compiler_params=pltpu.CompilerParams(
            collective_id=0, has_side_effects=True, vmem_limit_bytes=56 * 1024 * 1024
        ),
    )(prefix_of, weights, kv, queries, branch_keys, branch_values, attn_out, out_grad, lse)
    return (
        query_grad,
        key_grad,
        value_grad,
        pk.transpose(1, 0, 2),
        pv.transpose(1, 0, 2),
    )


def solution(mesh):
    placed = (
        P("br", None, "own"),
        P("br", None, "own"),
        P("br", None, "own"),
        P("br", None, "own"),
        P("br", None, "own"),
        P("br", "own", None),
        P("br", "own", None),
        P("br", "own", None),
        P("br"),
        P("br"),
    )
    return jax.shard_map(
        functools.partial(per_device, n_own=mesh.shape["own"], n_br=mesh.shape["br"]),
        mesh=mesh,
        in_specs=placed,
        out_specs=(
            P("br", None, "own"),
            P("br", None, "own"),
            P("br", None, "own"),
            P("br", "own", None),
            P("br", "own", None),
        ),
        check_vma=False,
    )
```

```python
import functools

import jax
import jax.numpy as jnp
from jax import lax
from jax.experimental import pallas as pl
from jax.experimental.pallas import tpu as pltpu
from jax.sharding import PartitionSpec as P

QH = 40
KVH = 8
HD = 128
GROUPS = QH // KVH
LOG2E = 1.4426950408889634
SCALE = HD ** (-0.5)
DEAD = 1e30

MESH = pl.DeviceIdType.MESH


def flip(index, bits):
    out, bit = index, 1
    while bit <= bits:
        if bits & bit:
            out = out + bit * (1 - 2 * ((index // bit) % 2))
        bit *= 2
    return out


def dot_nt(a, b):
    return lax.dot_general(a, b, (((1,), (1,)), ((), ())), preferred_element_type=jnp.float32)


def dot(a, b):
    return jnp.dot(a, b, preferred_element_type=jnp.float32)


def kernel(
    n_own,
    planes,
    pref_ref,
    count_ref,
    pkey_ref,
    pval_ref,
    lse_ref,
    q_hbm,
    bk_hbm,
    bv_hbm,
    ao_hbm,
    og_hbm,
    qg_ref,
    kg_ref,
    vg_ref,
    pk_ref,
    pv_ref,
    q_ref,
    bk_ref,
    bv_ref,
    ao_ref,
    og_ref,
    src,
    g0,
    g1,
    dqt,
    delta,
    lse2,
    acc,
    *rest,
):
    slots, length, _ = q_ref.shape
    kv_heads = bk_ref.shape[2] // HD
    cw = kv_heads * HD
    ppo, rows = src.shape[1], src.shape[2]
    num_pre = n_own * ppo
    half = planes // 2
    chunk_rows = half * 2 * rows
    own = lax.axis_index("own")
    br = lax.axis_index("br")
    plane, core = br // 2, br % 2
    gathered = (g0, g1)
    units = [(0, 0, kv_heads)] + [(1, k, k + 1) for k in range(kv_heads)]
    count = len(units)
    mine, outgoing, incoming, presum, land = (
        rest[i * count : (i + 1) * count] for i in range(5)
    )
    (
        load_sem,
        g_send,
        g_recv,
        f_send,
        f_recv,
        local_sem,
        s_send,
        s_recv,
        r_send,
        r_recv,
    ) = rest[5 * count :]

    def device(d, j):
        return {"own": flip(own, j), "br": flip(plane, d) * 2 + core}

    sibling = {"own": own, "br": plane * 2 + 1 - core}
    peers = [(d, j) for d in range(planes) for j in range(n_own) if (d, j) != (0, 0)]

    barrier = pltpu.get_barrier_semaphore()
    for d, j in peers:
        pl.semaphore_signal(barrier, inc=1, device_id=device(d, j), device_id_type=MESH)
    pl.semaphore_signal(barrier, inc=1, device_id=sibling, device_id_type=MESH)

    loads = [
        pltpu.make_async_copy(hbm, ref, load_sem.at[i])
        for i, (hbm, ref) in enumerate(
            (
                (og_hbm, og_ref),
                (ao_hbm, ao_ref),
                (q_hbm, q_ref),
                (bk_hbm, bk_ref),
                (bv_hbm, bv_ref),
            )
        )
    ]
    for load in loads:
        load.start()

    for o in range(n_own):
        for i in range(ppo):
            for k in range(kv_heads):
                start = o * cw + k * HD
                src[o, i, :, 2 * k * HD : (2 * k + 1) * HD] = pkey_ref[i, :, start : start + HD]
                src[o, i, :, (2 * k + 1) * HD : (2 * k + 2) * HD] = pval_ref[
                    i, :, start : start + HD
                ]

    pl.semaphore_wait(barrier, len(peers) + 1)

    def place(d, o, side):
        return gathered[d // half].at[pl.ds(o * ppo, ppo), 2 * (d % half) + side]

    def gather_copy(d, j):
        return pltpu.make_async_remote_copy(
            src_ref=src.at[flip(own, j)],
            dst_ref=place(d, own, 0),
            send_sem=g_send.at[d, j],
            recv_sem=g_recv.at[d, j],
            device_id=device(d, j),
            device_id_type=MESH,
        )

    def forward_copy(d, j):
        o = flip(own, j)
        return pltpu.make_async_remote_copy(
            src_ref=src.at[own] if (d, j) == (0, 0) else place(d, o, 0),
            dst_ref=place(d, o, 1),
            send_sem=f_send.at[d, j],
            recv_sem=f_recv.at[d, j],
            device_id=sibling,
            device_id_type=MESH,
        )

    for d, j in peers:
        gather_copy(d, j).start()
    forward_copy(0, 0).start()
    local = pltpu.make_async_copy(src.at[own], place(0, own, 0), local_sem)
    local.start()

    def head_cols(k, h):
        return pl.ds(pl.multiple_of(k * (GROUPS * HD) + h * HD, HD), HD)

    def kv_cols(k, base):
        return pl.ds(pl.multiple_of(base + k * HD, HD), HD)

    def pair_cols(k, second):
        return pl.ds(pl.multiple_of(k * (2 * HD) + second * HD, HD), HD)

    loads[0].wait()
    loads[1].wait()

    def prepare(step, carry):
        c, k = step // kv_heads, step % kv_heads
        dead = jnp.where(c < count_ref[0], 0.0, DEAD)
        for h in range(GROUPS):
            grad = og_ref[c, :, head_cols(k, h)].astype(jnp.float32)
            product = grad * ao_ref[c, :, head_cols(k, h)].astype(jnp.float32)
            delta[c, k, pl.ds(h, 1), :] = jnp.sum(product.T, axis=0, keepdims=True)
            lse2[c, k, pl.ds(h, 1), :] = lse_ref[c, pl.ds(k * GROUPS + h, 1), :] * LOG2E + dead
            dqt[c, k, h] = jnp.zeros((HD, length), jnp.float32)
        return carry

    lax.fori_loop(0, slots * kv_heads, prepare, 0)
    for load in loads[2:]:
        load.wait()

    def grads(c, k, key, val, causal):
        key_t = key.T
        dk = dv = None
        for h in range(GROUPS):
            query = q_ref[c, :, head_cols(k, h)]
            grad = og_ref[c, :, head_cols(k, h)]
            prob = jnp.exp2(
                dot_nt(key, query) * (SCALE * LOG2E) - lse2[c, k, pl.ds(h, 1), :]
            )
            if causal is not None:
                prob = jnp.where(causal, prob, 0.0)
            dscore = (prob * (dot_nt(val, grad) - delta[c, k, pl.ds(h, 1), :])).astype(
                jnp.bfloat16
            )
            dk_h = dot(dscore, query)
            dv_h = dot(prob.astype(jnp.bfloat16), grad)
            dk = dk_h if dk is None else dk + dk_h
            dv = dv_h if dv is None else dv + dv_h
            dqt[c, k, h] += dot(key_t, dscore)
        return dk * SCALE, dv

    def branch_step(step, carry):
        c, k = step // kv_heads, step % kv_heads
        causal = lax.broadcasted_iota(jnp.int32, (length, length), 0) <= lax.broadcasted_iota(
            jnp.int32, (length, length), 1
        )
        dk, dv = grads(c, k, bk_ref[c, :, kv_cols(k, 0)], bv_ref[c, :, kv_cols(k, 0)], causal)
        kg_ref[c, :, kv_cols(k, 0)] = dk.astype(jnp.bfloat16)
        vg_ref[c, :, kv_cols(k, 0)] = dv.astype(jnp.bfloat16)
        return carry

    def branch_steps(start, stop):
        lax.fori_loop(start, stop, branch_step, 0)

    def forward(chunk):
        for d, j in peers:
            if d // half == chunk:
                gather_copy(d, j).wait_recv()
                forward_copy(d, j).start()

    def forwarded(chunk):
        if chunk == 0:
            local.wait()
        for d in range(chunk * half, (chunk + 1) * half):
            for j in range(n_own):
                forward_copy(d, j).wait_recv()

    def prefix_unit(unit):
        chunk, first, last = units[unit]
        buf = gathered[chunk]

        def prefix_step(step, carry):
            c, k = step % slots, step // slots
            p = pref_ref[c]
            key = buf[p, :, :, pair_cols(k, 0)].reshape(chunk_rows, HD)
            val = buf[p, :, :, pair_cols(k, 1)].reshape(chunk_rows, HD)
            dk, dv = grads(c, k, key, val, None)
            acc[k, c, :, :HD] = dk
            acc[k, c, :, HD:] = dv
            return carry

        lax.fori_loop(first * slots, last * slots, prefix_step, 0)

        def combine(dd, carry):
            for k in range(first, last):
                cols = slice((k - first) * 2 * HD, (k - first + 1) * 2 * HD)
                for side in (0, 1):
                    start = pl.multiple_of((dd * 2 + side) * rows, rows)
                    parts = [acc[k, c, pl.ds(start, rows), :] for c in range(slots)]
                    for p in range(num_pre):
                        total = jnp.zeros_like(parts[0])
                        for c in range(slots):
                            total = total + parts[c] * jnp.where(pref_ref[c] == p, 1.0, 0.0)
                        if side == 0:
                            mine[unit][dd, p, :, cols] = total
                        else:
                            outgoing[unit][dd, p, :, cols] = total.astype(jnp.bfloat16)
            return carry

        lax.fori_loop(0, half, combine, 0)
        sibling_copy(unit).start()

    def sibling_copy(unit):
        return pltpu.make_async_remote_copy(
            src_ref=outgoing[unit],
            dst_ref=incoming[unit],
            send_sem=s_send.at[unit],
            recv_sem=s_recv.at[unit],
            device_id=sibling,
            device_id_type=MESH,
        )

    def reduce_copy(unit, d, j):
        return pltpu.make_async_remote_copy(
            src_ref=presum[unit].at[d % half, pl.ds(flip(own, j) * ppo, ppo)],
            dst_ref=land[unit].at[d % half, own],
            send_sem=r_send.at[unit, d % half, j],
            recv_sem=r_recv.at[unit, d % half, j],
            device_id=device(d, j),
            device_id_type=MESH,
        )

    reduce_copies = [
        (unit, d, j) for unit in range(count) for d, j in peers if d // half == units[unit][0]
    ]

    def send_sums(unit):
        sibling_copy(unit).wait_recv()

        def add(dd, carry):
            for p in range(num_pre):
                presum[unit][dd, p] = (
                    mine[unit][dd, p] + incoming[unit][dd, p].astype(jnp.float32)
                ).astype(jnp.bfloat16)
            return carry

        lax.fori_loop(0, half, add, 0)
        for u, d, j in reversed(reduce_copies):
            if u == unit:
                reduce_copy(u, d, j).start()
        if unit == 0:
            land[0][0, own] = presum[0][0, pl.ds(own * ppo, ppo)]

    steps = slots * kv_heads
    early, late = steps * 3 // 8, steps - kv_heads
    branch_steps(0, early)
    forward(0)
    forwarded(0)
    prefix_unit(0)
    branch_steps(early, late)
    send_sums(0)
    forward(1)
    forwarded(1)
    for unit in range(1, count):
        prefix_unit(unit)
        branch_steps(late + unit - 1, late + unit)
        send_sums(unit)

    def finish(step, carry):
        c, k = step // kv_heads, step % kv_heads
        for h in range(GROUPS):
            qg_ref[c, :, head_cols(k, h)] = (dqt[c, k, h] * SCALE).T.astype(jnp.bfloat16)
        return carry

    lax.fori_loop(0, steps, finish, 0)

    for u, d, j in reduce_copies:
        reduce_copy(u, d, j).wait_recv()
    for unit in range(1, count):
        _, first, last = units[unit]
        for k in range(first, last):
            far = slice((k - first) * 2 * HD, (k - first + 1) * 2 * HD)
            near = slice(k * 2 * HD, (k + 1) * 2 * HD)
            for o in range(n_own):
                for i in range(ppo):
                    total = jnp.zeros((rows, 2 * HD), jnp.float32)
                    for d in range(half):
                        total = total + land[0][d, o, i, :, near].astype(jnp.float32)
                        total = total + land[unit][d, o, i, :, far].astype(jnp.float32)
                    start = o * cw + k * HD
                    pk_ref[i, :, start : start + HD] = total[:, :HD].astype(jnp.bfloat16)
                    pv_ref[i, :, start : start + HD] = total[:, HD:].astype(jnp.bfloat16)

    forward_copy(0, 0).wait_send()
    for d, j in peers:
        gather_copy(d, j).wait_send()
        forward_copy(d, j).wait_send()
    for u, d, j in reduce_copies:
        reduce_copy(u, d, j).wait_send()
    for unit in range(count):
        sibling_copy(unit).wait_send()


def per_device(
    queries,
    branch_keys,
    branch_values,
    attn_out,
    out_grad,
    logsumexp,
    prefix_keys,
    prefix_values,
    prefix_of,
    counts,
    *,
    n_own,
    n_br,
):
    slots, length, _ = queries.shape
    cw = branch_keys.shape[2]
    kv_heads = cw // HD
    rows, ppo, full = prefix_keys.shape
    num_pre = n_own * ppo
    planes = n_br // 2
    half = planes // 2

    bf16, f32 = jnp.bfloat16, jnp.float32
    vmem = pl.BlockSpec(memory_space=pltpu.VMEM)
    smem = pl.BlockSpec(memory_space=pltpu.SMEM)
    hbm = pl.BlockSpec(memory_space=pl.ANY)
    dma = pltpu.SemaphoreType.DMA
    widths = [2 * cw] + [2 * HD] * kv_heads
    parts = [(half, num_pre, rows, width) for width in widths]
    lands = [(half, n_own, ppo, rows, width) for width in widths]
    query_grad, key_grad, value_grad, pk, pv = pl.pallas_call(
        functools.partial(kernel, n_own, planes),
        out_shape=(
            jax.ShapeDtypeStruct(queries.shape, bf16),
            jax.ShapeDtypeStruct(branch_keys.shape, bf16),
            jax.ShapeDtypeStruct(branch_keys.shape, bf16),
            jax.ShapeDtypeStruct((ppo, rows, full), bf16),
            jax.ShapeDtypeStruct((ppo, rows, full), bf16),
        ),
        in_specs=[smem, smem, vmem, vmem, vmem] + [hbm] * 5,
        out_specs=(vmem,) * 5,
        scratch_shapes=[
            pltpu.VMEM(queries.shape, bf16),
            pltpu.VMEM(branch_keys.shape, bf16),
            pltpu.VMEM(branch_keys.shape, bf16),
            pltpu.VMEM(queries.shape, bf16),
            pltpu.VMEM(queries.shape, bf16),
            pltpu.VMEM((n_own, ppo, rows, 2 * cw), bf16),
            pltpu.VMEM((num_pre, planes, rows, 2 * cw), bf16),
            pltpu.VMEM((num_pre, planes, rows, 2 * cw), bf16),
            pltpu.VMEM((slots, kv_heads, GROUPS, HD, length), f32),
            pltpu.VMEM((slots, kv_heads, GROUPS, length), f32),
            pltpu.VMEM((slots, kv_heads, GROUPS, length), f32),
            pltpu.VMEM((kv_heads, slots, planes * rows, 2 * HD), f32),
        ]
        + [pltpu.VMEM(part, f32) for part in parts]
        + [pltpu.VMEM(part, bf16) for part in parts] * 3
        + [pltpu.VMEM(block, bf16) for block in lands]
        + [
            dma((5,)),
            dma((planes, n_own)),
            dma((planes, n_own)),
            dma((planes, n_own)),
            dma((planes, n_own)),
            dma(()),
            dma((len(widths),)),
            dma((len(widths),)),
            dma((len(widths), half, n_own)),
            dma((len(widths), half, n_own)),
        ],
        compiler_params=pltpu.CompilerParams(
            collective_id=0, has_side_effects=True, vmem_limit_bytes=56 * 1024 * 1024
        ),
    )(
        prefix_of,
        counts,
        prefix_keys.transpose(1, 0, 2),
        prefix_values.transpose(1, 0, 2),
        logsumexp,
        queries,
        branch_keys,
        branch_values,
        attn_out,
        out_grad,
    )
    return (
        query_grad,
        key_grad,
        value_grad,
        pk.transpose(1, 0, 2),
        pv.transpose(1, 0, 2),
    )


def solution(mesh):
    placed = (
        P("br", None, "own"),
        P("br", None, "own"),
        P("br", None, "own"),
        P("br", None, "own"),
        P("br", None, "own"),
        P("br", "own", None),
        P("br", "own", None),
        P("br", "own", None),
        P("br"),
        P("br"),
    )
    return jax.shard_map(
        functools.partial(per_device, n_own=mesh.shape["own"], n_br=mesh.shape["br"]),
        mesh=mesh,
        in_specs=placed,
        out_specs=(
            P("br", None, "own"),
            P("br", None, "own"),
            P("br", None, "own"),
            P("br", "own", None),
            P("br", "own", None),
        ),
        check_vma=False,
    )
```

```python
import functools

import jax
import jax.numpy as jnp
from jax import lax
from jax.experimental import pallas as pl
from jax.experimental.pallas import tpu as pltpu
from jax.sharding import PartitionSpec as P

QH = 40
KVH = 8
HD = 128
GROUPS = QH // KVH
LOG2E = 1.4426950408889634
SCALE = HD ** (-0.5)
DEAD = 1e30

MESH = pl.DeviceIdType.MESH


def flip(index, bits):
    out, bit = index, 1
    while bit <= bits:
        if bits & bit:
            out = out + bit * (1 - 2 * ((index // bit) % 2))
        bit *= 2
    return out


def dot_nt(a, b):
    return lax.dot_general(a, b, (((1,), (1,)), ((), ())), preferred_element_type=jnp.float32)


def dot(a, b):
    return jnp.dot(a, b, preferred_element_type=jnp.float32)


def kernel(
    n_own,
    planes,
    pref_ref,
    count_ref,
    pkey_ref,
    pval_ref,
    lse_ref,
    q_hbm,
    bk_hbm,
    bv_hbm,
    ao_hbm,
    og_hbm,
    qg_hbm,
    kg_hbm,
    vg_hbm,
    pk_ref,
    pv_ref,
    qg_ref,
    kg_ref,
    vg_ref,
    q_ref,
    bk_ref,
    bv_ref,
    ao_ref,
    og_ref,
    src,
    g0,
    g1,
    dqt,
    delta,
    lse2,
    acc,
    *rest,
):
    slots, length, _ = q_ref.shape
    kv_heads = bk_ref.shape[2] // HD
    cw = kv_heads * HD
    ppo, rows = src.shape[1], src.shape[2]
    num_pre = n_own * ppo
    half = planes // 2
    chunk_rows = half * 2 * rows
    own = lax.axis_index("own")
    br = lax.axis_index("br")
    plane, core = br // 2, br % 2
    gathered = (g0, g1)
    units = [(0, 0, kv_heads)] + [(1, k, k + 1) for k in range(kv_heads)]
    count = len(units)
    mine, outgoing, incoming, presum, land, hops, total_b = (
        rest[i * count : (i + 1) * count] for i in range(7)
    )
    (
        load_sem,
        g_send,
        g_recv,
        f_send,
        f_recv,
        local_sem,
        s_send,
        s_recv,
        r_send,
        r_recv,
        h_send,
        h_recv,
        store_sem,
    ) = rest[7 * count :]

    def device(d, j):
        return {"own": flip(own, j), "br": flip(plane, d) * 2 + core}

    sibling = {"own": own, "br": plane * 2 + 1 - core}
    blocks = [(d, j) for d in range(planes) for j in range(n_own) if (d, j) != (0, 0)]
    peers = [(d, j) for d, j in blocks if d <= half]

    barrier = pltpu.get_barrier_semaphore()
    for d, j in peers:
        pl.semaphore_signal(barrier, inc=1, device_id=device(d, j), device_id_type=MESH)
    pl.semaphore_signal(barrier, inc=1, device_id=sibling, device_id_type=MESH)

    loads = [
        pltpu.make_async_copy(hbm, ref, load_sem.at[i])
        for i, (hbm, ref) in enumerate(
            (
                (og_hbm, og_ref),
                (ao_hbm, ao_ref),
                (q_hbm, q_ref),
                (bk_hbm, bk_ref),
                (bv_hbm, bv_ref),
            )
        )
    ]
    for load in loads:
        load.start()

    for o in range(n_own):
        for i in range(ppo):
            for k in range(kv_heads):
                start = o * cw + k * HD
                src[o, i, :, 2 * k * HD : (2 * k + 1) * HD] = pkey_ref[i, :, start : start + HD]
                src[o, i, :, (2 * k + 1) * HD : (2 * k + 2) * HD] = pval_ref[
                    i, :, start : start + HD
                ]

    pl.semaphore_wait(barrier, len(peers) + 1)

    def place(d, o, side):
        return gathered[d // half].at[pl.ds(o * ppo, ppo), 2 * (d % half) + side]

    def gather_copy(d, j):
        o = flip(own, j)
        relay = d > half
        return pltpu.make_async_remote_copy(
            src_ref=place(half, o, 0) if relay else src.at[o],
            dst_ref=place(d, o if relay else own, 0),
            send_sem=g_send.at[d, j],
            recv_sem=g_recv.at[d, j],
            device_id=device(d - half, 0) if relay else device(d, j),
            device_id_type=MESH,
        )

    def forward_copy(d, j):
        o = flip(own, j)
        return pltpu.make_async_remote_copy(
            src_ref=src.at[own] if (d, j) == (0, 0) else place(d, o, 0),
            dst_ref=place(d, o, 1),
            send_sem=f_send.at[d, j],
            recv_sem=f_recv.at[d, j],
            device_id=sibling,
            device_id_type=MESH,
        )

    for d, j in peers:
        gather_copy(d, j).start()
    forward_copy(0, 0).start()
    local = pltpu.make_async_copy(src.at[own], place(0, own, 0), local_sem)
    local.start()

    def head_cols(k, h):
        return pl.ds(pl.multiple_of(k * (GROUPS * HD) + h * HD, HD), HD)

    def kv_cols(k, base):
        return pl.ds(pl.multiple_of(base + k * HD, HD), HD)

    def pair_cols(k, second):
        return pl.ds(pl.multiple_of(k * (2 * HD) + second * HD, HD), HD)

    loads[0].wait()
    loads[1].wait()

    def prepare(step, carry):
        c, k = step // kv_heads, step % kv_heads
        dead = jnp.where(c < count_ref[0], 0.0, DEAD)
        for h in range(GROUPS):
            grad = og_ref[c, :, head_cols(k, h)].astype(jnp.float32)
            product = grad * ao_ref[c, :, head_cols(k, h)].astype(jnp.float32)
            delta[c, k, pl.ds(h, 1), :] = jnp.sum(product.T, axis=0, keepdims=True)
            lse2[c, k, pl.ds(h, 1), :] = lse_ref[k * GROUPS + h, pl.ds(c, 1), :] * LOG2E + dead
            dqt[c, k, h] = jnp.zeros((HD, length), jnp.float32)
        return carry

    lax.fori_loop(0, slots * kv_heads, prepare, 0)
    for load in loads[2:]:
        load.wait()

    def grads(c, k, key, val, causal):
        key_t = key.T
        dk = dv = None
        for h in range(GROUPS):
            query = q_ref[c, :, head_cols(k, h)]
            grad = og_ref[c, :, head_cols(k, h)]
            prob = jnp.exp2(
                dot_nt(key, query) * (SCALE * LOG2E) - lse2[c, k, pl.ds(h, 1), :]
            )
            if causal is not None:
                prob = jnp.where(causal, prob, 0.0)
            dscore = (prob * (dot_nt(val, grad) - delta[c, k, pl.ds(h, 1), :])).astype(
                jnp.bfloat16
            )
            dk_h = dot(dscore, query)
            dv_h = dot(prob.astype(jnp.bfloat16), grad)
            dk = dk_h if dk is None else dk + dk_h
            dv = dv_h if dv is None else dv + dv_h
            dqt[c, k, h] += dot(key_t, dscore)
        return dk * SCALE, dv

    def branch_step(step, carry):
        c, k = step // kv_heads, step % kv_heads
        causal = lax.broadcasted_iota(jnp.int32, (length, length), 0) <= lax.broadcasted_iota(
            jnp.int32, (length, length), 1
        )
        dk, dv = grads(c, k, bk_ref[c, :, kv_cols(k, 0)], bv_ref[c, :, kv_cols(k, 0)], causal)
        kg_ref[c, :, kv_cols(k, 0)] = dk.astype(jnp.bfloat16)
        vg_ref[c, :, kv_cols(k, 0)] = dv.astype(jnp.bfloat16)
        return carry

    def branch_steps(start, stop):
        lax.fori_loop(start, stop, branch_step, 0)

    def forward(first, last):
        for d, j in blocks:
            if first <= d < last:
                gather_copy(d, j).wait_recv()
                if d == half:
                    for e in range(1, half):
                        gather_copy(half + e, j).start()
                forward_copy(d, j).start()

    def forwarded(chunk):
        if chunk == 0:
            local.wait()
        for d in range(chunk * half, (chunk + 1) * half):
            for j in range(n_own):
                forward_copy(d, j).wait_recv()

    def prefix_unit(unit):
        chunk, first, last = units[unit]
        buf = gathered[chunk]

        def prefix_step(step, carry):
            c, k = step % slots, step // slots
            p = pref_ref[c]
            key = buf[p, :, :, pair_cols(k, 0)].reshape(chunk_rows, HD)
            val = buf[p, :, :, pair_cols(k, 1)].reshape(chunk_rows, HD)
            dk, dv = grads(c, k, key, val, None)
            acc[k, c, :, :HD] = dk
            acc[k, c, :, HD:] = dv
            return carry

        lax.fori_loop(first * slots, (first + 1) * slots, prefix_step, 0)
        if chunk == 0:
            forward(half, half + 1)
        if last > first + 1:
            lax.fori_loop((first + 1) * slots, last * slots, prefix_step, 0)

        def combine(dd, carry):
            for k in range(first, last):
                cols = slice((k - first) * 2 * HD, (k - first + 1) * 2 * HD)
                for side in (0, 1):
                    start = pl.multiple_of((dd * 2 + side) * rows, rows)
                    parts = [acc[k, c, pl.ds(start, rows), :] for c in range(slots)]
                    for p in range(num_pre):
                        total = jnp.zeros_like(parts[0])
                        for c in range(slots):
                            total = total + parts[c] * jnp.where(pref_ref[c] == p, 1.0, 0.0)
                        if side == 0:
                            mine[unit][dd, p, :, cols] = total
                        else:
                            outgoing[unit][dd, p, :, cols] = total.astype(jnp.bfloat16)
            return carry

        lax.fori_loop(0, half, combine, 0)
        sibling_copy(unit).start()

    def sibling_copy(unit):
        return pltpu.make_async_remote_copy(
            src_ref=outgoing[unit],
            dst_ref=incoming[unit],
            send_sem=s_send.at[unit],
            recv_sem=s_recv.at[unit],
            device_id=sibling,
            device_id_type=MESH,
        )

    def reduce_copy(unit, d, j):
        o = flip(own, j)
        if unit == 0:
            source, target = presum[0].at[d, pl.ds(o * ppo, ppo)], land[0].at[d, own]
        else:
            source, target = total_b[unit].at[pl.ds(o * ppo, ppo)], land[unit].at[0, own]
        return pltpu.make_async_remote_copy(
            src_ref=source,
            dst_ref=target,
            send_sem=r_send.at[unit, d % half, j],
            recv_sem=r_recv.at[unit, d % half, j],
            device_id=device(d, j),
            device_id_type=MESH,
        )

    def hop_copy(unit, e):
        return pltpu.make_async_remote_copy(
            src_ref=presum[unit].at[e],
            dst_ref=hops[unit].at[e - 1],
            send_sem=h_send.at[unit, e],
            recv_sem=h_recv.at[unit, e],
            device_id=device(e, 0),
            device_id_type=MESH,
        )

    reduce_copies = [
        (unit, d, j) for unit in range(count) for d, j in peers if d // half == units[unit][0]
    ]

    def send_near():
        sibling_copy(0).wait_recv()

        def add(dd, carry):
            for p in range(num_pre):
                presum[0][dd, p] = (
                    mine[0][dd, p] + incoming[0][dd, p].astype(jnp.float32)
                ).astype(jnp.bfloat16)
            return carry

        lax.fori_loop(0, half, add, 0)
        for u, d, j in reversed(reduce_copies):
            if u == 0:
                reduce_copy(u, d, j).start()
        land[0][0, own] = presum[0][0, pl.ds(own * ppo, ppo)]

    def send_hops(unit):
        sibling_copy(unit).wait_recv()
        for e in range(1, half):
            for p in range(num_pre):
                presum[unit][e, p] = (
                    mine[unit][e, p] + incoming[unit][e, p].astype(jnp.float32)
                ).astype(jnp.bfloat16)
            hop_copy(unit, e).start()

    def send_far(unit):
        for e in range(1, half):
            hop_copy(unit, e).wait_recv()
        for p in range(num_pre):
            total = mine[unit][0, p] + incoming[unit][0, p].astype(jnp.float32)
            for e in range(1, half):
                total = total + hops[unit][e - 1, p].astype(jnp.float32)
            total_b[unit][p] = total.astype(jnp.bfloat16)
        for u, d, j in reduce_copies:
            if u == unit:
                reduce_copy(u, d, j).start()

    steps = slots * kv_heads
    early, late = steps * 3 // 8, steps - kv_heads
    branch_steps(0, early)
    forward(0, half)
    forwarded(0)
    prefix_unit(0)
    branch_steps(early, late)
    send_near()
    forward(half + 1, planes)
    forwarded(1)
    for unit in range(1, count):
        prefix_unit(unit)
        if unit > 1:
            send_far(unit - 1)
        branch_steps(late + unit - 1, late + unit)
        send_hops(unit)

    def finish(step, carry):
        c, k = step // kv_heads, step % kv_heads
        for h in range(GROUPS):
            qg_ref[c, :, head_cols(k, h)] = (dqt[c, k, h] * SCALE).T.astype(jnp.bfloat16)
        return carry

    lax.fori_loop(0, steps, finish, 0)
    stores = [
        pltpu.make_async_copy(ref, out, store_sem.at[i])
        for i, (ref, out) in enumerate(((qg_ref, qg_hbm), (kg_ref, kg_hbm), (vg_ref, vg_hbm)))
    ]
    for store in stores:
        store.start()
    send_far(count - 1)

    for u, d, j in reduce_copies:
        reduce_copy(u, d, j).wait_recv()
    for unit in range(1, count):
        _, first, last = units[unit]
        for k in range(first, last):
            far = slice((k - first) * 2 * HD, (k - first + 1) * 2 * HD)
            near = slice(k * 2 * HD, (k + 1) * 2 * HD)
            for o in range(n_own):
                for i in range(ppo):
                    total = jnp.zeros((rows, 2 * HD), jnp.float32)
                    for d in range(half):
                        total = total + land[0][d, o, i, :, near].astype(jnp.float32)
                    total = total + land[unit][0, o, i, :, far].astype(jnp.float32)
                    start = o * cw + k * HD
                    pk_ref[i, :, start : start + HD] = total[:, :HD].astype(jnp.bfloat16)
                    pv_ref[i, :, start : start + HD] = total[:, HD:].astype(jnp.bfloat16)

    forward_copy(0, 0).wait_send()
    for d, j in blocks:
        gather_copy(d, j).wait_send()
        forward_copy(d, j).wait_send()
    for unit in range(1, count):
        for e in range(1, half):
            hop_copy(unit, e).wait_send()
    for store in stores:
        store.wait()
    for u, d, j in reduce_copies:
        reduce_copy(u, d, j).wait_send()
    for unit in range(count):
        sibling_copy(unit).wait_send()


def copy_kernel(*refs):
    count = (len(refs) - 1) // 2
    sems = refs[-1]
    copies = []
    for source, target in zip(refs[:count], refs[count : 2 * count]):
        pieces = source.shape[0] if len(source.shape) == 3 else 1
        for i in range(pieces):
            copies.append(
                pltpu.make_async_copy(source.at[i], target.at[i], sems.at[len(copies)])
            )
    for copy in copies:
        copy.start()
    for copy in copies:
        copy.wait()


def write_out(arrays):
    any_spec = pl.BlockSpec(memory_space=pl.ANY)
    pieces = sum(array.shape[0] for array in arrays)
    return pl.pallas_call(
        copy_kernel,
        out_shape=tuple(jax.ShapeDtypeStruct(a.shape, a.dtype) for a in arrays),
        in_specs=[any_spec] * len(arrays),
        out_specs=(any_spec,) * len(arrays),
        scratch_shapes=[pltpu.SemaphoreType.DMA((pieces,))],
        compiler_params=pltpu.CompilerParams(vmem_limit_bytes=60 * 1024 * 1024),
    )(*arrays)


def per_device(
    queries,
    branch_keys,
    branch_values,
    attn_out,
    out_grad,
    logsumexp,
    prefix_keys,
    prefix_values,
    prefix_of,
    counts,
    *,
    n_own,
    n_br,
):
    slots, length, _ = queries.shape
    cw = branch_keys.shape[2]
    kv_heads = cw // HD
    rows, ppo, full = prefix_keys.shape
    num_pre = n_own * ppo
    planes = n_br // 2
    half = planes // 2

    bf16, f32 = jnp.bfloat16, jnp.float32
    vmem = pl.BlockSpec(memory_space=pltpu.VMEM)
    smem = pl.BlockSpec(memory_space=pltpu.SMEM)
    hbm = pl.BlockSpec(memory_space=pl.ANY)
    dma = pltpu.SemaphoreType.DMA
    widths = [2 * cw] + [2 * HD] * kv_heads
    parts = [(half, num_pre, rows, width) for width in widths]
    lands = [
        (half if unit == 0 else 1, n_own, ppo, rows, width) for unit, width in enumerate(widths)
    ]
    hops = [(max(half - 1, 1), num_pre, rows, width) for width in widths]
    totals = [(num_pre, rows, width) for width in widths]
    grads = pl.pallas_call(
        functools.partial(kernel, n_own, planes),
        out_shape=(
            jax.ShapeDtypeStruct(queries.shape, bf16),
            jax.ShapeDtypeStruct(branch_keys.shape, bf16),
            jax.ShapeDtypeStruct(branch_keys.shape, bf16),
            jax.ShapeDtypeStruct((ppo, rows, full), bf16),
            jax.ShapeDtypeStruct((ppo, rows, full), bf16),
        ),
        in_specs=[smem, smem, vmem, vmem, vmem] + [hbm] * 5,
        out_specs=(hbm,) * 3 + (vmem,) * 2,
        scratch_shapes=[
            pltpu.VMEM(queries.shape, bf16),
            pltpu.VMEM(branch_keys.shape, bf16),
            pltpu.VMEM(branch_keys.shape, bf16),
            pltpu.VMEM(queries.shape, bf16),
            pltpu.VMEM(branch_keys.shape, bf16),
            pltpu.VMEM(branch_keys.shape, bf16),
            pltpu.VMEM(queries.shape, bf16),
            pltpu.VMEM(queries.shape, bf16),
            pltpu.VMEM((n_own, ppo, rows, 2 * cw), bf16),
            pltpu.VMEM((num_pre, planes, rows, 2 * cw), bf16),
            pltpu.VMEM((num_pre, planes, rows, 2 * cw), bf16),
            pltpu.VMEM((slots, kv_heads, GROUPS, HD, length), f32),
            pltpu.VMEM((slots, kv_heads, GROUPS, length), f32),
            pltpu.VMEM((slots, kv_heads, GROUPS, length), f32),
            pltpu.VMEM((kv_heads, slots, planes * rows, 2 * HD), f32),
        ]
        + [pltpu.VMEM(part, f32) for part in parts]
        + [pltpu.VMEM(part, bf16) for part in parts] * 3
        + [pltpu.VMEM(block, bf16) for block in lands + hops + totals]
        + [
            dma((5,)),
            dma((planes, n_own)),
            dma((planes, n_own)),
            dma((planes, n_own)),
            dma((planes, n_own)),
            dma(()),
            dma((len(widths),)),
            dma((len(widths),)),
            dma((len(widths), half, n_own)),
            dma((len(widths), half, n_own)),
            dma((len(widths), half)),
            dma((len(widths), half)),
            dma((3,)),
        ],
        compiler_params=pltpu.CompilerParams(
            collective_id=0, has_side_effects=True, vmem_limit_bytes=56 * 1024 * 1024
        ),
    )(
        prefix_of,
        counts,
        prefix_keys.transpose(1, 0, 2),
        prefix_values.transpose(1, 0, 2),
        logsumexp.transpose(1, 0, 2),
        queries,
        branch_keys,
        branch_values,
        attn_out,
        out_grad,
    )
    query_grad, key_grad, value_grad, pk, pv = write_out(grads)
    return (
        query_grad,
        key_grad,
        value_grad,
        pk.transpose(1, 0, 2),
        pv.transpose(1, 0, 2),
    )


def solution(mesh):
    placed = (
        P("br", None, "own"),
        P("br", None, "own"),
        P("br", None, "own"),
        P("br", None, "own"),
        P("br", None, "own"),
        P("br", "own", None),
        P("br", "own", None),
        P("br", "own", None),
        P("br"),
        P("br"),
    )
    return jax.shard_map(
        functools.partial(per_device, n_own=mesh.shape["own"], n_br=mesh.shape["br"]),
        mesh=mesh,
        in_specs=placed,
        out_specs=(
            P("br", None, "own"),
            P("br", None, "own"),
            P("br", None, "own"),
            P("br", "own", None),
            P("br", "own", None),
        ),
        check_vma=False,
    )
```

```python
import functools

import jax
import jax.numpy as jnp
from jax import lax
from jax.experimental import pallas as pl
from jax.experimental.pallas import tpu as pltpu
from jax.sharding import PartitionSpec as P

QH = 40
KVH = 8
HD = 128
GROUPS = QH // KVH
LOG2E = 1.4426950408889634
SCALE = HD ** (-0.5)
DEAD = 1e30

MESH = pl.DeviceIdType.MESH


def flip(index, bits):
    out, bit = index, 1
    while bit <= bits:
        if bits & bit:
            out = out + bit * (1 - 2 * ((index // bit) % 2))
        bit *= 2
    return out


def dot_nt(a, b):
    return lax.dot_general(a, b, (((1,), (1,)), ((), ())), preferred_element_type=jnp.float32)


def dot(a, b):
    return jnp.dot(a, b, preferred_element_type=jnp.float32)


def kernel(
    n_own,
    planes,
    pref_ref,
    count_ref,
    pkey_ref,
    pval_ref,
    lse_ref,
    q_hbm,
    bk_hbm,
    bv_hbm,
    ao_hbm,
    og_hbm,
    qg_hbm,
    kg_hbm,
    vg_hbm,
    pk_ref,
    pv_ref,
    qg_ref,
    kg_ref,
    vg_ref,
    q_ref,
    bk_ref,
    bv_ref,
    ao_ref,
    og_ref,
    src,
    g0,
    g1,
    dqt,
    delta,
    lse2,
    acc,
    *rest,
):
    slots, length, _ = q_ref.shape
    kv_heads = bk_ref.shape[2] // HD
    cw = kv_heads * HD
    ppo, rows = src.shape[1], src.shape[2]
    num_pre = n_own * ppo
    half = planes // 2
    chunk_rows = half * 2 * rows
    own = lax.axis_index("own")
    br = lax.axis_index("br")
    plane, core = br // 2, br % 2
    gathered = (g0, g1)
    units = [(0, 0, kv_heads)] + [(1, k, k + 1) for k in range(kv_heads)]
    count = len(units)
    mine, outgoing, incoming, presum, land, hops, total_b = (
        rest[i * count : (i + 1) * count] for i in range(7)
    )
    (
        load_sem,
        g_send,
        g_recv,
        f_send,
        f_recv,
        local_sem,
        s_send,
        s_recv,
        r_send,
        r_recv,
        h_send,
        h_recv,
        store_sem,
    ) = rest[7 * count :]

    def device(d, j):
        return {"own": flip(own, j), "br": flip(plane, d) * 2 + core}

    sibling = {"own": own, "br": plane * 2 + 1 - core}
    blocks = [(d, j) for d in range(planes) for j in range(n_own) if (d, j) != (0, 0)]
    peers = [(d, j) for d, j in blocks if d <= half]

    barrier = pltpu.get_barrier_semaphore()
    for d, j in peers:
        pl.semaphore_signal(barrier, inc=1, device_id=device(d, j), device_id_type=MESH)
    pl.semaphore_signal(barrier, inc=1, device_id=sibling, device_id_type=MESH)

    loads = [
        pltpu.make_async_copy(hbm, ref, load_sem.at[i])
        for i, (hbm, ref) in enumerate(
            (
                (og_hbm, og_ref),
                (ao_hbm, ao_ref),
                (q_hbm, q_ref),
                (bk_hbm, bk_ref),
                (bv_hbm, bv_ref),
            )
        )
    ]
    for load in loads:
        load.start()

    for o in range(n_own):
        for i in range(ppo):
            for k in range(kv_heads):
                start = o * cw + k * HD
                src[o, i, :, 2 * k * HD : (2 * k + 1) * HD] = pkey_ref[i, :, start : start + HD]
                src[o, i, :, (2 * k + 1) * HD : (2 * k + 2) * HD] = pval_ref[
                    i, :, start : start + HD
                ]

    pl.semaphore_wait(barrier, len(peers) + 1)

    def place(d, o, side):
        return gathered[d // half].at[pl.ds(o * ppo, ppo), 2 * (d % half) + side]

    def gather_copy(d, j):
        o = flip(own, j)
        relay = d > half
        return pltpu.make_async_remote_copy(
            src_ref=place(half, o, 0) if relay else src.at[o],
            dst_ref=place(d, o if relay else own, 0),
            send_sem=g_send.at[d, j],
            recv_sem=g_recv.at[d, j],
            device_id=device(d - half, 0) if relay else device(d, j),
            device_id_type=MESH,
        )

    def forward_copy(d, j):
        o = flip(own, j)
        return pltpu.make_async_remote_copy(
            src_ref=src.at[own] if (d, j) == (0, 0) else place(d, o, 0),
            dst_ref=place(d, o, 1),
            send_sem=f_send.at[d, j],
            recv_sem=f_recv.at[d, j],
            device_id=sibling,
            device_id_type=MESH,
        )

    for d, j in peers:
        gather_copy(d, j).start()
    forward_copy(0, 0).start()
    local = pltpu.make_async_copy(src.at[own], place(0, own, 0), local_sem)
    local.start()

    def head_cols(k, h):
        return pl.ds(pl.multiple_of(k * (GROUPS * HD) + h * HD, HD), HD)

    def kv_cols(k, base):
        return pl.ds(pl.multiple_of(base + k * HD, HD), HD)

    def pair_cols(k, second):
        return pl.ds(pl.multiple_of(k * (2 * HD) + second * HD, HD), HD)

    loads[0].wait()
    loads[1].wait()

    def prepare(step, carry):
        c, k = step // kv_heads, step % kv_heads
        dead = jnp.where(c < count_ref[0], 0.0, DEAD)
        for h in range(GROUPS):
            grad = og_ref[c, :, head_cols(k, h)].astype(jnp.float32)
            product = grad * ao_ref[c, :, head_cols(k, h)].astype(jnp.float32)
            delta[c, k, pl.ds(h, 1), :] = jnp.sum(product.T, axis=0, keepdims=True)
            lse2[c, k, pl.ds(h, 1), :] = lse_ref[k * GROUPS + h, pl.ds(c, 1), :] * LOG2E + dead
            dqt[c, k, h] = jnp.zeros((HD, length), jnp.float32)
        return carry

    lax.fori_loop(0, slots * kv_heads, prepare, 0)
    for load in loads[2:]:
        load.wait()

    def grads(c, k, key, val, causal):
        key_t = key.T
        dk = dv = None
        for h in range(GROUPS):
            query = q_ref[c, :, head_cols(k, h)]
            grad = og_ref[c, :, head_cols(k, h)]
            prob = jnp.exp2(
                dot_nt(key, query) * (SCALE * LOG2E) - lse2[c, k, pl.ds(h, 1), :]
            )
            if causal is not None:
                prob = jnp.where(causal, prob, 0.0)
            dscore = (prob * (dot_nt(val, grad) - delta[c, k, pl.ds(h, 1), :])).astype(
                jnp.bfloat16
            )
            dk_h = dot(dscore, query)
            dv_h = dot(prob.astype(jnp.bfloat16), grad)
            dk = dk_h if dk is None else dk + dk_h
            dv = dv_h if dv is None else dv + dv_h
            dqt[c, k, h] += dot(key_t, dscore)
        return dk * SCALE, dv

    def branch_step(step, carry):
        c, k = step // kv_heads, step % kv_heads
        causal = lax.broadcasted_iota(jnp.int32, (length, length), 0) <= lax.broadcasted_iota(
            jnp.int32, (length, length), 1
        )
        dk, dv = grads(c, k, bk_ref[c, :, kv_cols(k, 0)], bv_ref[c, :, kv_cols(k, 0)], causal)
        kg_ref[c, :, kv_cols(k, 0)] = dk.astype(jnp.bfloat16)
        vg_ref[c, :, kv_cols(k, 0)] = dv.astype(jnp.bfloat16)
        return carry

    def branch_steps(start, stop):
        lax.fori_loop(start, stop, branch_step, 0)

    def forward(first, last):
        for d, j in blocks:
            if first <= d < last:
                gather_copy(d, j).wait_recv()
                if d == half:
                    for e in range(1, half):
                        gather_copy(half + e, j).start()
                forward_copy(d, j).start()

    def forwarded(chunk):
        if chunk == 0:
            local.wait()
        for d in range(chunk * half, (chunk + 1) * half):
            for j in range(n_own):
                forward_copy(d, j).wait_recv()

    def prefix_unit(unit):
        chunk, first, last = units[unit]
        buf = gathered[chunk]

        def prefix_step(step, carry):
            c, k = step % slots, step // slots
            p = pref_ref[c]
            key = buf[p, :, :, pair_cols(k, 0)].reshape(chunk_rows, HD)
            val = buf[p, :, :, pair_cols(k, 1)].reshape(chunk_rows, HD)
            dk, dv = grads(c, k, key, val, None)
            acc[k, c, :, :HD] = dk
            acc[k, c, :, HD:] = dv
            return carry

        lax.fori_loop(first * slots, (first + 1) * slots, prefix_step, 0)
        if chunk == 0:
            forward(half, half + 1)
        if last > first + 1:
            lax.fori_loop((first + 1) * slots, last * slots, prefix_step, 0)

        def combine(dd, carry):
            for k in range(first, last):
                cols = slice((k - first) * 2 * HD, (k - first + 1) * 2 * HD)
                for side in (0, 1):
                    start = pl.multiple_of((dd * 2 + side) * rows, rows)
                    parts = [acc[k, c, pl.ds(start, rows), :] for c in range(slots)]
                    for p in range(num_pre):
                        total = jnp.zeros_like(parts[0])
                        for c in range(slots):
                            total = total + parts[c] * jnp.where(pref_ref[c] == p, 1.0, 0.0)
                        if side == 0:
                            mine[unit][dd, p, :, cols] = total
                        else:
                            outgoing[unit][dd, p, :, cols] = total.astype(jnp.bfloat16)
            return carry

        lax.fori_loop(0, half, combine, 0)
        sibling_copy(unit).start()

    def sibling_copy(unit):
        return pltpu.make_async_remote_copy(
            src_ref=outgoing[unit],
            dst_ref=incoming[unit],
            send_sem=s_send.at[unit],
            recv_sem=s_recv.at[unit],
            device_id=sibling,
            device_id_type=MESH,
        )

    def reduce_copy(unit, d, j):
        o = flip(own, j)
        if unit == 0:
            source, target = presum[0].at[d, pl.ds(o * ppo, ppo)], land[0].at[d, own]
        else:
            source, target = total_b[unit].at[pl.ds(o * ppo, ppo)], land[unit].at[0, own]
        return pltpu.make_async_remote_copy(
            src_ref=source,
            dst_ref=target,
            send_sem=r_send.at[unit, d % half, j],
            recv_sem=r_recv.at[unit, d % half, j],
            device_id=device(d, j),
            device_id_type=MESH,
        )

    def hop_copy(unit, e):
        return pltpu.make_async_remote_copy(
            src_ref=presum[unit].at[e],
            dst_ref=hops[unit].at[e - 1],
            send_sem=h_send.at[unit, e],
            recv_sem=h_recv.at[unit, e],
            device_id=device(e, 0),
            device_id_type=MESH,
        )

    reduce_copies = [
        (unit, d, j) for unit in range(count) for d, j in peers if d // half == units[unit][0]
    ]

    def send_near():
        sibling_copy(0).wait_recv()

        def add(dd, carry):
            for p in range(num_pre):
                presum[0][dd, p] = (
                    mine[0][dd, p] + incoming[0][dd, p].astype(jnp.float32)
                ).astype(jnp.bfloat16)
            return carry

        lax.fori_loop(0, half, add, 0)
        for u, d, j in reversed(reduce_copies):
            if u == 0:
                reduce_copy(u, d, j).start()
        land[0][0, own] = presum[0][0, pl.ds(own * ppo, ppo)]

    def send_hops(unit):
        sibling_copy(unit).wait_recv()
        for e in range(1, half):
            for p in range(num_pre):
                presum[unit][e, p] = (
                    mine[unit][e, p] + incoming[unit][e, p].astype(jnp.float32)
                ).astype(jnp.bfloat16)
            hop_copy(unit, e).start()

    def send_far(unit):
        for e in range(1, half):
            hop_copy(unit, e).wait_recv()
        for p in range(num_pre):
            total = mine[unit][0, p] + incoming[unit][0, p].astype(jnp.float32)
            for e in range(1, half):
                total = total + hops[unit][e - 1, p].astype(jnp.float32)
            total_b[unit][p] = total.astype(jnp.bfloat16)
        for u, d, j in reduce_copies:
            if u == unit:
                reduce_copy(u, d, j).start()

    steps = slots * kv_heads
    early, late = steps * 3 // 8, steps - kv_heads
    branch_steps(0, early)
    forward(0, half)
    forwarded(0)
    prefix_unit(0)
    branch_steps(early, late)
    send_near()
    forward(half + 1, planes)
    forwarded(1)
    for unit in range(1, count):
        prefix_unit(unit)
        if unit > 1:
            send_far(unit - 1)
        branch_steps(late + unit - 1, late + unit)
        send_hops(unit)

    def finish(step, carry):
        c, k = step // kv_heads, step % kv_heads
        for h in range(GROUPS):
            qg_ref[c, :, head_cols(k, h)] = (dqt[c, k, h] * SCALE).T.astype(jnp.bfloat16)
        return carry

    lax.fori_loop(0, steps, finish, 0)
    stores = [
        pltpu.make_async_copy(ref, out, store_sem.at[i])
        for i, (ref, out) in enumerate(((qg_ref, qg_hbm), (kg_ref, kg_hbm), (vg_ref, vg_hbm)))
    ]
    for store in stores:
        store.start()
    send_far(count - 1)

    for u, d, j in reduce_copies:
        reduce_copy(u, d, j).wait_recv()
    for unit in range(1, count):
        _, first, last = units[unit]
        for k in range(first, last):
            far = slice((k - first) * 2 * HD, (k - first + 1) * 2 * HD)
            near = slice(k * 2 * HD, (k + 1) * 2 * HD)
            for o in range(n_own):
                for i in range(ppo):
                    total = jnp.zeros((rows, 2 * HD), jnp.float32)
                    for d in range(half):
                        total = total + land[0][d, o, i, :, near].astype(jnp.float32)
                    total = total + land[unit][0, o, i, :, far].astype(jnp.float32)
                    start = o * cw + k * HD
                    pk_ref[i, :, start : start + HD] = total[:, :HD].astype(jnp.bfloat16)
                    pv_ref[i, :, start : start + HD] = total[:, HD:].astype(jnp.bfloat16)

    forward_copy(0, 0).wait_send()
    for d, j in blocks:
        gather_copy(d, j).wait_send()
        forward_copy(d, j).wait_send()
    for unit in range(1, count):
        for e in range(1, half):
            hop_copy(unit, e).wait_send()
    for store in stores:
        store.wait()
    for u, d, j in reduce_copies:
        reduce_copy(u, d, j).wait_send()
    for unit in range(count):
        sibling_copy(unit).wait_send()


def copy_kernel(*refs):
    count = (len(refs) - 2) // 3
    read_sems, write_sems = refs[-2:]
    reads, writes = [], []
    for source, target, held in zip(
        refs[:count], refs[count : 2 * count], refs[2 * count : 3 * count]
    ):
        for i in range(source.shape[0]):
            n = len(reads)
            reads.append(pltpu.make_async_copy(source.at[i], held.at[i], read_sems.at[n]))
            writes.append(pltpu.make_async_copy(held.at[i], target.at[i], write_sems.at[n]))
    for read in reads:
        read.start()
    for read, write in zip(reads, writes):
        read.wait()
        write.start()
    for write in writes:
        write.wait()


def write_out(arrays):
    any_spec = pl.BlockSpec(memory_space=pl.ANY)
    pieces = sum(array.shape[0] for array in arrays)
    return pl.pallas_call(
        copy_kernel,
        out_shape=tuple(jax.ShapeDtypeStruct(a.shape, a.dtype) for a in arrays),
        in_specs=[any_spec] * len(arrays),
        out_specs=(any_spec,) * len(arrays),
        scratch_shapes=[pltpu.VMEM(a.shape, a.dtype) for a in arrays]
        + [pltpu.SemaphoreType.DMA((pieces,))] * 2,
        compiler_params=pltpu.CompilerParams(vmem_limit_bytes=60 * 1024 * 1024),
    )(*arrays)


def per_device(
    queries,
    branch_keys,
    branch_values,
    attn_out,
    out_grad,
    logsumexp,
    prefix_keys,
    prefix_values,
    prefix_of,
    counts,
    *,
    n_own,
    n_br,
):
    slots, length, _ = queries.shape
    cw = branch_keys.shape[2]
    kv_heads = cw // HD
    rows, ppo, full = prefix_keys.shape
    num_pre = n_own * ppo
    planes = n_br // 2
    half = planes // 2

    bf16, f32 = jnp.bfloat16, jnp.float32
    vmem = pl.BlockSpec(memory_space=pltpu.VMEM)
    smem = pl.BlockSpec(memory_space=pltpu.SMEM)
    hbm = pl.BlockSpec(memory_space=pl.ANY)
    dma = pltpu.SemaphoreType.DMA
    widths = [2 * cw] + [2 * HD] * kv_heads
    parts = [(half, num_pre, rows, width) for width in widths]
    lands = [
        (half if unit == 0 else 1, n_own, ppo, rows, width) for unit, width in enumerate(widths)
    ]
    hops = [(max(half - 1, 1), num_pre, rows, width) for width in widths]
    totals = [(num_pre, rows, width) for width in widths]
    grads = pl.pallas_call(
        functools.partial(kernel, n_own, planes),
        out_shape=(
            jax.ShapeDtypeStruct(queries.shape, bf16),
            jax.ShapeDtypeStruct(branch_keys.shape, bf16),
            jax.ShapeDtypeStruct(branch_keys.shape, bf16),
            jax.ShapeDtypeStruct((ppo, rows, full), bf16),
            jax.ShapeDtypeStruct((ppo, rows, full), bf16),
        ),
        in_specs=[smem, smem, vmem, vmem, vmem] + [hbm] * 5,
        out_specs=(hbm,) * 3 + (vmem,) * 2,
        scratch_shapes=[
            pltpu.VMEM(queries.shape, bf16),
            pltpu.VMEM(branch_keys.shape, bf16),
            pltpu.VMEM(branch_keys.shape, bf16),
            pltpu.VMEM(queries.shape, bf16),
            pltpu.VMEM(branch_keys.shape, bf16),
            pltpu.VMEM(branch_keys.shape, bf16),
            pltpu.VMEM(queries.shape, bf16),
            pltpu.VMEM(queries.shape, bf16),
            pltpu.VMEM((n_own, ppo, rows, 2 * cw), bf16),
            pltpu.VMEM((num_pre, planes, rows, 2 * cw), bf16),
            pltpu.VMEM((num_pre, planes, rows, 2 * cw), bf16),
            pltpu.VMEM((slots, kv_heads, GROUPS, HD, length), f32),
            pltpu.VMEM((slots, kv_heads, GROUPS, length), f32),
            pltpu.VMEM((slots, kv_heads, GROUPS, length), f32),
            pltpu.VMEM((kv_heads, slots, planes * rows, 2 * HD), f32),
        ]
        + [pltpu.VMEM(part, f32) for part in parts]
        + [pltpu.VMEM(part, bf16) for part in parts] * 3
        + [pltpu.VMEM(block, bf16) for block in lands + hops + totals]
        + [
            dma((5,)),
            dma((planes, n_own)),
            dma((planes, n_own)),
            dma((planes, n_own)),
            dma((planes, n_own)),
            dma(()),
            dma((len(widths),)),
            dma((len(widths),)),
            dma((len(widths), half, n_own)),
            dma((len(widths), half, n_own)),
            dma((len(widths), half)),
            dma((len(widths), half)),
            dma((3,)),
        ],
        compiler_params=pltpu.CompilerParams(
            collective_id=0, has_side_effects=True, vmem_limit_bytes=56 * 1024 * 1024
        ),
    )(
        prefix_of,
        counts,
        prefix_keys.transpose(1, 0, 2),
        prefix_values.transpose(1, 0, 2),
        logsumexp.transpose(1, 0, 2),
        queries,
        branch_keys,
        branch_values,
        attn_out,
        out_grad,
    )
    query_grad, key_grad, value_grad, pk, pv = write_out(grads)
    return (
        query_grad,
        key_grad,
        value_grad,
        pk.transpose(1, 0, 2),
        pv.transpose(1, 0, 2),
    )


def solution(mesh):
    placed = (
        P("br", None, "own"),
        P("br", None, "own"),
        P("br", None, "own"),
        P("br", None, "own"),
        P("br", None, "own"),
        P("br", "own", None),
        P("br", "own", None),
        P("br", "own", None),
        P("br"),
        P("br"),
    )
    return jax.shard_map(
        functools.partial(per_device, n_own=mesh.shape["own"], n_br=mesh.shape["br"]),
        mesh=mesh,
        in_specs=placed,
        out_specs=(
            P("br", None, "own"),
            P("br", None, "own"),
            P("br", None, "own"),
            P("br", "own", None),
            P("br", "own", None),
        ),
        check_vma=False,
    )
```
